128 devices in a mesh: dp: 16 (over y, x_hi, core), tensor: 8 (over z, x_lo).
Axes of the slice: x: 4 (x_hi: 2, x_lo: 2; x = x_hi * 2 + x_lo), y: 4, z: 4, core: 2. Of those that a mesh axis runs over, the one named last changes fastest.
Arguments:
- queries_a: bfloat16 [2048, 8192], P('dp', 'tensor'), may hold values from -32 to 32
- keys_a: bfloat16 [2048, 1024], P('dp', 'tensor'), may hold values from -4 to 4
- values_a: bfloat16 [2048, 1024], P('dp', 'tensor'), may hold values from -5 to 5
- queries_b: bfloat16 [2048, 8192], P('dp', 'tensor'), may hold values from -32 to 32
- keys_b: bfloat16 [2048, 1024], P('dp', 'tensor'), may hold values from -4 to 4
- values_b: bfloat16 [2048, 1024], P('dp', 'tensor'), may hold values from -5 to 5
- out_a: bfloat16 [8192, 8192], P('tensor', 'dp'), may hold values from -12 to 12
- out_b: bfloat16 [8192, 8192], P('tensor', 'dp'), may hold values from -12 to 12
- lengths: int32 [16, 4], P('dp'), may hold values from 1 to 64, 128 in all within a row
Outputs:
- merged: float32 [8192, 8192], P('tensor', 'dp')
- residual: float32 [8192, 8192], P('tensor', 'dp')
The draws below stay inside these ranges and needn't reach their ends.
All inputs are finite; a program needn't handle non-finite values.
Results may differ from the reference program's by a relative error of at most 0.023.
Values may be sent and summed in bfloat16 or wider, within the bound.
No kernel may reach another device: no remote copies, remote signals or barrier semaphores. Data moves between devices by JAX's collectives and lax.ppermute only.
A program may use at most 64 MiB of HBM per device.

```python
import math
import jax
import jax.numpy as jnp
import numpy as np
from jax import lax

D = 8192
HQ = 64
KVH = 8
HD = 128
TOK_DEV = 128
SEQS = 4
MOST = 64
SHARDS = 16
TOKENS = 2048
N_TENSOR = 8


def draw_key_rows(key, tag):
    base_key = jax.random.fold_in(key, tag)
    normal_rows = jnp.clip(jax.random.normal(base_key, (TOKENS, KVH * HD), jnp.float32), -4.0, 4.0)
    rows = normal_rows
    return rows


def draw_query_rows(key, tag):
    noise_key = jax.random.fold_in(key, tag + 50)
    normal_rows = jnp.clip(jax.random.normal(noise_key, (TOKENS, HQ * HD), jnp.float32), -4.0, 4.0)
    noise = normal_rows
    return noise


def shared_base(key):
    return jnp.clip(jax.random.normal(jax.random.fold_in(key, 7), (HQ * HD, D), jnp.float32), -4.0, 4.0)


def column_ramp():
    column = jnp.arange(D).astype(jnp.float32) / (D - 1)
    return 0.5 * jnp.exp(math.log(3.0) * column)[None, :]


def draw_keys_a(key, part):
    rows = draw_key_rows(key, 101)
    return rows.astype(jnp.bfloat16)


def draw_queries_a(key, part):
    rows = draw_query_rows(key, 101)
    return rows.astype(jnp.bfloat16)


def draw_keys_b(key, part):
    rows = draw_key_rows(key, 202)
    return rows.astype(jnp.bfloat16)


def draw_queries_b(key, part):
    rows = draw_query_rows(key, 202)
    return rows.astype(jnp.bfloat16)


def draw_out_a(key, part):
    base = shared_base(key)
    key = jax.random.fold_in(key, 8)
    noise = jnp.clip(jax.random.normal(key, (HQ * HD, D), jnp.float32), -4.0, 4.0)
    ramp = column_ramp()
    return (base + ramp * noise).astype(jnp.bfloat16)


def draw_out_b(key, part):
    base = shared_base(key)
    key = jax.random.fold_in(key, 9)
    noise = jnp.clip(jax.random.normal(key, (HQ * HD, D), jnp.float32), -4.0, 4.0)
    ramp = column_ramp()
    return (base + ramp * noise).astype(jnp.bfloat16)


def block_scale(stream_key, extent, shards, low, high):
    def one(axis_at, parts):
        draws = jax.random.uniform(jax.random.fold_in(jax.random.fold_in(stream_key, 6), axis_at), (parts,), jnp.float32, low / len(shards), high / len(shards))
        return jnp.repeat(jnp.exp(draws), extent[axis_at] // parts).reshape((-1,) + (1,) * (len(extent) - axis_at - 1))

    factor_of = one(*shards[0])
    for cut in shards[1:]:
        factor_of = factor_of * one(*cut)
    return factor_of


def length_profile(count, total, limit, lean):
    weights = [(1 << 20) // math.isqrt(grade ** lean) + 1 for grade in range(2, count + 1)]
    rest, holding = total - limit - (count - 1), [1] * (count - 1)
    while rest > 0:
        free = [i for i in range(count - 1) if holding[i] < limit]
        whole, remaining = sum([weights[i] for i in free]), rest
        for i in free:
            addition = min(limit - holding[i], max(1, remaining * weights[i] // whole), rest)
            holding[i] = holding[i] + addition
            rest = rest - addition
    return np.array([limit] + holding)


def ragged_sizes(key, count, total, bound, lean):
    if count == 2:
        one = jax.random.randint(key, (), max(1, total - bound), min(bound, total - 1) + 1)
        return jnp.stack([one, total - one])
    tallies = jnp.asarray(length_profile(count, total, bound, lean), jnp.int32)
    couples = (count - 1) // 2
    donor, receiver = tallies[1:1 + 2 * couples:2], tallies[2:2 + 2 * couples:2]
    slack = jnp.minimum(donor - 1, bound - receiver)
    moved = jax.random.randint(jax.random.fold_in(key, 1), (couples,), 0, 1 << 20) % (slack + 1)
    tallies = tallies.at[1:1 + 2 * couples:2].set(donor - moved).at[2:2 + 2 * couples:2].set(receiver + moved)
    return tallies[jax.random.permutation(jax.random.fold_in(key, 2), count)]


def scatter_about(rng, shape, deviation, limit, shards=(), kind=jnp.bfloat16):
    level = block_scale(rng, shape, shards, -0.22, 0.18) if shards else 1.0
    values = jax.random.normal(rng, shape, jnp.float32) * deviation * level
    return jnp.minimum(jnp.maximum(values, -limit), limit).astype(kind)


def setup_inputs(seed: int = 0) -> dict:
    splits = jax.random.split(jax.random.key(seed), 10)
    return {
        "queries_a": draw_queries_a(jax.random.fold_in(splits[9], 71), 0),
        "keys_a": draw_keys_a(jax.random.fold_in(splits[9], 71), 0),
        "values_a": scatter_about(splits[2], (TOKENS, KVH * HD), 1.0, 5.0, ((0, 16), (1, 8))),
        "queries_b": draw_queries_b(jax.random.fold_in(splits[9], 71), 0),
        "keys_b": draw_keys_b(jax.random.fold_in(splits[9], 71), 0),
        "values_b": scatter_about(splits[5], (TOKENS, KVH * HD), 1.0, 5.0, ((0, 16), (1, 8))),
        "out_a": draw_out_a(jax.random.fold_in(splits[9], 71), 0),
        "out_b": draw_out_b(jax.random.fold_in(splits[9], 71), 0),
        "lengths": jax.vmap(lambda own: ragged_sizes(own, SEQS, TOK_DEV, MOST, 2))(jax.random.split(splits[8], SHARDS)).reshape((SHARDS, SEQS)).astype(jnp.int32),
    }


damping = 0.05

def group_outputs(queries, keys, values, lengths):
    positions = jnp.arange(TOK_DEV)
    group_size = HQ // KVH

    def one_group(items):
        query_block, key_block, value_block, seq_lengths = items
        ends = jnp.cumsum(seq_lengths)
        segment = lax.optimization_barrier(jnp.sum((positions[:, None] >= ends[None, :]).astype(jnp.int32), axis=1))
        allowed = (segment[:, None] == segment[None, :]) & (positions[None, :] <= positions[:, None])
        query_heads = query_block.reshape(TOK_DEV, HQ, HD).astype(jnp.float32)
        key_heads = jnp.repeat(key_block.reshape(TOK_DEV, KVH, HD).astype(jnp.float32), group_size, axis=1)
        value_heads = jnp.repeat(value_block.reshape(TOK_DEV, KVH, HD).astype(jnp.float32), group_size, axis=1)
        scores = jnp.einsum('qhd,khd->hqk', query_heads, key_heads) / math.sqrt(HD)
        scores = jnp.where(allowed[None], scores, jnp.float32(-1e+30))
        top = lax.optimization_barrier(jnp.max(scores, axis=2, keepdims=True))
        exps = jnp.where(allowed[None], jnp.exp(scores - top), jnp.float32(0.0))
        weights = (exps / lax.optimization_barrier(jnp.sum(exps, axis=2, keepdims=True))).astype(jnp.bfloat16)
        mixed = jnp.einsum('hqk,khd->qhd', weights.astype(jnp.float32), value_heads)
        return mixed.astype(jnp.bfloat16).reshape(TOK_DEV, HQ * HD)
    result = lax.map(one_group, (queries.reshape(SHARDS, TOK_DEV, HQ * HD), keys.reshape(SHARDS, TOK_DEV, KVH * HD), values.reshape(SHARDS, TOK_DEV, KVH * HD), lengths))
    return result.reshape(TOKENS, HQ * HD)

def pull_back(outputs, tangent):
    return jnp.dot(outputs.T, tangent, preferred_element_type=jnp.float32)

def push_forward(outputs, direction):
    group_width = HQ * HD // N_TENSOR
    total = jnp.zeros((outputs.shape[0], direction.shape[1]), jnp.float32)
    for group in range(N_TENSOR):
        columns = outputs[:, group * group_width:(group + 1) * group_width]
        rows = direction[group * group_width:(group + 1) * group_width, :]
        partial_low = jnp.dot(columns, rows, preferred_element_type=jnp.float32).astype(jnp.bfloat16)
        total = total + partial_low.astype(jnp.float32)
    return total.astype(jnp.bfloat16)

def reference(queries_a, keys_a, values_a, queries_b, keys_b, values_b, out_a, out_b, lengths):
    outputs_a = group_outputs(queries_a, keys_a, values_a, lengths)
    outputs_b = group_outputs(queries_b, keys_b, values_b, lengths)
    first = out_a.astype(jnp.float32)
    second = out_b.astype(jnp.float32)
    midpoint = (first + second) * 0.5
    half_gap = (first - second) * 0.5
    gap_low = half_gap.astype(jnp.bfloat16)
    tangent_a = push_forward(outputs_a, gap_low)
    tangent_b = push_forward(outputs_b, gap_low)
    residual_start = (pull_back(outputs_a, tangent_a) - pull_back(outputs_b, tangent_b)) / TOKENS
    res_norm = jnp.sum(residual_start * residual_start)
    direction_low = residual_start.astype(jnp.bfloat16)
    probe_a = push_forward(outputs_a, direction_low)
    probe_b = push_forward(outputs_b, direction_low)
    curvature = (pull_back(outputs_a, probe_a) + pull_back(outputs_b, probe_b)) / TOKENS + damping * residual_start
    energy = jnp.sum(residual_start * curvature)
    step_size = res_norm / energy
    return (midpoint + step_size * residual_start, residual_start - step_size * curvature)
```

```python
import math

import jax
import jax.numpy as jnp
from jax import lax
from jax.sharding import Mesh, PartitionSpec as P

HD = 128
damping = 0.05
AXES = ("y", "xh", "c", "z", "xl")


def attend(queries, keys, values, segment, positions):
    row_count = queries.shape[0]
    head_count = queries.shape[1] // HD
    kv_heads = keys.shape[1] // HD
    group_size = head_count // kv_heads
    query_heads = queries.reshape(row_count, kv_heads, group_size, HD)
    key_heads = keys.reshape(row_count, kv_heads, HD)
    value_heads = values.reshape(row_count, kv_heads, HD)
    allowed = (segment[:, None] == segment[None, :]) & (positions[None, :] <= positions[:, None])
    scores = jnp.einsum(
        "qkgd,skd->kgqs", query_heads, key_heads, preferred_element_type=jnp.float32
    ) / math.sqrt(HD)
    scores = jnp.where(allowed[None, None], scores, jnp.float32(-1e30))
    top = jnp.max(scores, axis=3, keepdims=True)
    exps = jnp.where(allowed[None, None], jnp.exp(scores - top), jnp.float32(0.0))
    weights = (exps / jnp.sum(exps, axis=3, keepdims=True)).astype(jnp.bfloat16)
    mixed = jnp.einsum("kgqs,skd->qkgd", weights, value_heads, preferred_element_type=jnp.float32)
    return mixed.astype(jnp.bfloat16).reshape(row_count, head_count * HD)


def ring(value, axis, shift):
    return lax.ppermute(value, axis, [(i, (i + shift) % 4) for i in range(4)])


def swap(value, axis):
    return lax.ppermute(value, axis, [(0, 1), (1, 0)])


def far(value):
    return lax.ppermute(value, ("xh", "xl"), [(i, 3 - i) for i in range(4)])


def gather_outputs(own):
    half = own.shape[0] // 2
    quarter = own.shape[0] // 4

    def both(block):
        return jnp.concatenate([block, swap(block, "c")], axis=0)

    def wide(mine, partners):
        return both(jnp.concatenate([mine, partners], axis=1))

    s = swap(own, "xl")
    o = far(own)
    up = ring(own, "y", 1)
    down = ring(own, "y", -1)
    s_up = swap(up, "xl")
    o_down = far(down)
    o_up = ring(o, "y", 1)
    s_down = ring(s, "y", -1)
    opp_up = swap(o_up, "xl")
    opp_down = far(s_down)
    s_two = ring(s_up, "y", 1)
    o_two = ring(o_down, "y", -1)
    opp = jnp.concatenate([swap(o[:half], "xl"), far(s[half:])], axis=0)
    two = jnp.concatenate([ring(up[:half], "y", 1), ring(down[half:], "y", -1)], axis=0)
    opp_two = jnp.concatenate(
        [
            swap(o_two[:quarter], "xl"),
            far(s_two[quarter : 2 * quarter]),
            ring(opp_up[2 * quarter : 3 * quarter], "y", 1),
            ring(opp_down[3 * quarter :], "y", -1),
        ],
        axis=0,
    )
    return [
        wide(own, s),
        jnp.concatenate([wide(up, s_up), wide(down, s_down)], axis=0),
        jnp.concatenate([wide(opp_up, o_up), wide(opp_down, o_down)], axis=0),
        jnp.concatenate([wide(opp, o), wide(two, s_two), wide(opp_two, o_two)], axis=0),
    ]


def reduce_share(partial, z):
    share = partial.shape[0] // 4
    pieces = partial.reshape(4, share, partial.shape[1])
    total = lax.dynamic_index_in_dim(pieces, z, 0, keepdims=False).astype(jnp.float32)
    for k in (1, 2, 3):
        piece = lax.dynamic_index_in_dim(pieces, (z + k) % 4, 0, keepdims=False)
        total = total + ring(piece, "z", k).astype(jnp.float32)
    return total


def spread_share(share, z):
    one, two, three = ring(share, "z", 1), ring(share, "z", 2), ring(share, "z", 3)
    rows = share.shape[0]
    line = jnp.concatenate([three, two, one, share, three, two, one], axis=0)
    return lax.dynamic_slice_in_dim(line, (3 - z) * rows, 4 * rows, axis=0)


def sum_all(value):
    for axis in ("z", ("xh", "xl"), "y"):
        value = value + ring(value, axis, 1) + ring(value, axis, 2) + ring(value, axis, 3)
    return value + swap(value, "c")


def pull_back(outputs, tangent):
    return lax.dot_general(
        outputs, tangent, (((0,), (0,)), ((), ())), preferred_element_type=jnp.float32
    )


def push(outputs, direction):
    return jnp.dot(outputs, direction, preferred_element_type=jnp.float32).astype(jnp.bfloat16)


def shards(queries_a, keys_a, values_a, queries_b, keys_b, values_b, out_a, out_b, lengths):
    z, xl = lax.axis_index("z"), lax.axis_index("xl")
    token_total = 16 * queries_a.shape[0]
    rows, width = out_a.shape[0], out_a.shape[1] // 2
    first = out_a.astype(jnp.float32)
    second = out_b.astype(jnp.float32)
    midpoint = (first + second) * 0.5
    gap_low = ((first - second) * 0.5).astype(jnp.bfloat16)
    left, right = gap_low[:, :width], gap_low[:, width:]
    gap = jnp.concatenate(
        [jnp.where(xl == 0, left, right), swap(jnp.where(xl == 0, right, left), "xl")], axis=0
    )

    positions = jnp.arange(queries_a.shape[0])
    ends = jnp.cumsum(lengths[0])
    segment = jnp.sum((positions[:, None] >= ends[None, :]).astype(jnp.int32), axis=1)
    local_a = attend(queries_a, keys_a, values_a, segment, positions)
    local_b = attend(queries_b, keys_b, values_b, segment, positions)
    chunks = gather_outputs(jnp.concatenate([local_a, local_b], axis=0))

    residual_start = 0.0
    for chunk in chunks:
        share = reduce_share(push(chunk, gap), z).astype(jnp.bfloat16)
        tangent = spread_share(share, z)
        is_b = (jnp.arange(tangent.shape[0]) // queries_a.shape[0]) % 2 == 1
        residual_start = residual_start + pull_back(chunk, jnp.where(is_b[:, None], -tangent, tangent))
    residual_start = residual_start / token_total
    direction_low = residual_start.astype(jnp.bfloat16)
    other_start = swap(direction_low[rows:], "xl")

    shares = [reduce_share(push(chunk, direction_low), z) for chunk in chunks]
    squares = jnp.stack(
        [jnp.sum(residual_start * residual_start), sum(jnp.sum(share * share) for share in shares)]
    )
    totals = sum_all(jnp.broadcast_to(squares[:, None], (2, 128)))
    res_norm = totals[0, 0]
    energy = totals[1, 0] / token_total + damping * res_norm
    step_size = res_norm / energy

    curvature = 0.0
    for chunk, share in zip(chunks, shares):
        curvature = curvature + pull_back(chunk, spread_share(share.astype(jnp.bfloat16), z))
    curvature = curvature / token_total + damping * residual_start
    residual = residual_start - step_size * curvature
    other_residual = swap(residual[rows:].astype(jnp.bfloat16), "xl").astype(jnp.float32)

    def place(mine, other):
        return jnp.where(
            xl == 0,
            jnp.concatenate([mine, other], axis=1),
            jnp.concatenate([other, mine], axis=1),
        )

    start = place(residual_start[:rows], other_start.astype(jnp.float32))
    return (midpoint + step_size * start, place(residual[:rows], other_residual))


def solution(mesh):
    fine = Mesh(mesh.devices.reshape(4, 2, 2, 4, 2), AXES)
    dp, tensor = ("y", "xh", "c"), ("z", "xl")
    tokens = P(dp, tensor)
    return jax.shard_map(
        shards,
        mesh=fine,
        in_specs=(tokens,) * 6 + (P(tensor, dp),) * 2 + (P(dp, None),),
        out_specs=(P(tensor, dp), P(tensor, dp)),
        check_vma=False,
    )
```

```python
import math

import jax
import jax.numpy as jnp
from jax import lax
from jax.experimental import pallas as pl
from jax.experimental.pallas import tpu as pltpu
from jax.sharding import Mesh, PartitionSpec as P

HD = 128
HEADS = 8
TOK = 128
FOLD = 64
damping = 0.05
AXES = ("y", "xh", "c", "z", "xl")
PLANE = ("y", "xh", "c", "xl")
V_ROW = HEADS * TOK
END_ROW = V_ROW + 2 * TOK
ROWS = END_ROW + 16
HOPS = (0, 1, 3, 2)


def attend_kernel(lengths, qa, ka, va, qb, kb, vb, out):
    first = lengths[0, 0]
    second = first + lengths[0, 1]
    third = second + lengths[0, 2]

    def end_of(key):
        return jnp.where(
            key < first,
            first - 1,
            jnp.where(key < second, second - 1, jnp.where(key < third, third - 1, TOK - 1)),
        )

    key = lax.broadcasted_iota(jnp.int32, (TOK, TOK), 1)
    query = lax.broadcasted_iota(jnp.int32, (TOK, TOK), 0)
    allowed = (key <= query) & (query <= end_of(key))

    def folded(q_ref, k_ref, head):
        scores = lax.dot_general(
            q_ref[:, head * HD : (head + 1) * HD],
            k_ref[...],
            (((1,), (1,)), ((), ())),
            preferred_element_type=jnp.float32,
        ) / math.sqrt(HD)
        scores = jnp.where(allowed, scores, jnp.float32(-1e30))
        top = jnp.max(scores, axis=1, keepdims=True)
        exps = jnp.where(allowed, jnp.exp(scores - top), jnp.float32(0.0))
        weights = exps / jnp.sum(exps, axis=1, keepdims=True)
        return weights + pltpu.roll(weights, FOLD, 1)

    for head in range(HEADS):
        out[head * TOK : (head + 1) * TOK, :] = jnp.where(
            key < FOLD, folded(qa, ka, head), folded(qb, kb, head)
        ).astype(jnp.bfloat16)
    out[V_ROW : V_ROW + TOK, :] = va[...]
    out[V_ROW + TOK : END_ROW, :] = vb[...]
    lane = lax.broadcasted_iota(jnp.int32, (16, TOK), 1) & (FOLD - 1)
    row = lax.broadcasted_iota(jnp.int32, (16, TOK), 0)
    ends = end_of(jnp.where(row < 8, lane, lane + FOLD))
    out[END_ROW:, :] = ends.astype(jnp.float32).astype(jnp.bfloat16)


def attend(lengths, *operands):
    def whole(shape):
        return pl.BlockSpec(shape, lambda i: (0, 0))

    return pl.pallas_call(
        attend_kernel,
        out_shape=jax.ShapeDtypeStruct((ROWS, TOK), jnp.bfloat16),
        grid=(1,),
        in_specs=[pl.BlockSpec(memory_space=pltpu.SMEM)] + [whole(o.shape) for o in operands],
        out_specs=whole((ROWS, TOK)),
        compiler_params=pltpu.CompilerParams(vmem_limit_bytes=60 << 20),
        cost_estimate=pl.CostEstimate(flops=1, bytes_accessed=1, transcendentals=0),
    )(lengths, *operands)


def unpack_kernel(place, slot, column, block, *refs):
    out = refs[-1]
    ends = block[END_ROW:, :].astype(jnp.float32)
    end_low, end_high = ends[0:1, :].astype(jnp.int32), ends[8:9, :].astype(jnp.int32)
    key = lax.broadcasted_iota(jnp.int32, (TOK, TOK), 1) & (FOLD - 1)
    query = lax.broadcasted_iota(jnp.int32, (TOK, TOK), 0)
    low = jnp.where((key <= query) & (query <= end_low), 1.0, 0.0).astype(jnp.bfloat16)
    high = jnp.where((key + FOLD <= query) & (query <= end_high), 1.0, 0.0).astype(jnp.bfloat16)
    packed = block[:V_ROW, :].reshape(HEADS, TOK, TOK)
    weights = jnp.concatenate(
        [(packed * low[None]).reshape(V_ROW, TOK), (packed * high[None]).reshape(V_ROW, TOK)], axis=1
    )
    va, vb = block[V_ROW : V_ROW + TOK, :], block[V_ROW + TOK : END_ROW, :]
    none = jnp.zeros((FOLD, HD), jnp.bfloat16)
    values = jnp.concatenate(
        [
            jnp.concatenate([va[:FOLD], none], axis=1),
            jnp.concatenate([none, vb[:FOLD]], axis=1),
            jnp.concatenate([va[FOLD:], none], axis=1),
            jnp.concatenate([none, vb[FOLD:]], axis=1),
        ],
        axis=0,
    )
    mixed = jnp.dot(weights, values, preferred_element_type=jnp.float32).astype(jnp.bfloat16)
    for head in range(HEADS):
        part = mixed[head * TOK : (head + 1) * TOK, :]
        out[0, 0, 0, :, head * HD : (head + 1) * HD] = part[:, :HD]
        out[0, 1, 0, :, head * HD : (head + 1) * HD] = part[:, HD:]


def unpack(blocks, place, slot, column, before):
    count = blocks.shape[0] // ROWS
    return pl.pallas_call(
        unpack_kernel,
        out_shape=jax.ShapeDtypeStruct((4, 2, 2, TOK, 2 * HEADS * HD), jnp.bfloat16),
        grid_spec=pltpu.PrefetchScalarGridSpec(
            num_scalar_prefetch=3,
            grid=(count,),
            in_specs=[pl.BlockSpec((ROWS, TOK), lambda i, p, s, c: (i, 0))]
            + [pl.BlockSpec(memory_space=pl.ANY)] * len(before),
            out_specs=pl.BlockSpec(
                (1, 2, 1, TOK, HEADS * HD), lambda i, p, s, c: (p[i], 0, s[i], 0, c[i])
            ),
        ),
        input_output_aliases={4: 0} if before else {},
        compiler_params=pltpu.CompilerParams(vmem_limit_bytes=16 << 20),
        cost_estimate=pl.CostEstimate(flops=1, bytes_accessed=1, transcendentals=0),
    )(place, slot, column, blocks, *before)


def finish_kernel(
    column, sums, out_a, out_b, start, curvature, other_start, other_curvature, merged, residual
):
    norm = jnp.sum(sums[:, 0, :])
    step = norm / (jnp.sum(sums[:, 1, :]) / (16 * TOK) + damping * norm)
    midpoint = (out_a[...].astype(jnp.float32) + out_b[...].astype(jnp.float32)) * 0.5

    def write(begin, image):
        merged[...] = midpoint + step * begin
        residual[...] = begin - step * image

    @pl.when(pl.program_id(0) == 0)
    def _():
        write(start[...], curvature[...])

    @pl.when(pl.program_id(0) == 1)
    def _():
        write(other_start[...].astype(jnp.float32), other_curvature[...].astype(jnp.float32))


def finish(xl, sums, out_a, out_b, start, curvature, other_start, other_curvature):
    rows, width = other_start.shape
    tile = rows // 2
    placed = pl.BlockSpec((tile, width), lambda i, r, x: (r, (i + x[0]) % 2))
    mine = pl.BlockSpec((tile, width), lambda i, r, x: (jnp.where(i == 0, r, 1), 0))
    other = pl.BlockSpec((tile, width), lambda i, r, x: (jnp.where(i == 0, 0, r), 0))
    shape = jax.ShapeDtypeStruct((rows, 2 * width), jnp.float32)
    return pl.pallas_call(
        finish_kernel,
        out_shape=[shape, shape],
        grid_spec=pltpu.PrefetchScalarGridSpec(
            num_scalar_prefetch=1,
            grid=(2, 2),
            in_specs=[pl.BlockSpec(sums.shape, lambda i, r, x: (0, 0, 0)), placed, placed, mine, mine, other, other],
            out_specs=[placed, placed],
        ),
        compiler_params=pltpu.CompilerParams(vmem_limit_bytes=56 << 20),
        cost_estimate=pl.CostEstimate(flops=1, bytes_accessed=1, transcendentals=0),
    )(
        xl.reshape(1),
        sums,
        out_a,
        out_b,
        start,
        curvature,
        other_start,
        other_curvature,
    )


def ring(value, axis, shift):
    return lax.ppermute(value, axis, [(i, (i + shift) % 4) for i in range(4)])


def swap(value, axis):
    return lax.ppermute(value, axis, [(0, 1), (1, 0)])


def plane_step(value, stage, hop):
    def index(y, x, c):
        return ((y * 2 + x // 2) * 2 + c) * 2 + x % 2

    pairs = []
    for y in range(4):
        for x in range(4):
            for c in range(2):
                along_x = (stage + c) % 2 == 0
                to = ((y, x ^ hop) if along_x else (y ^ hop, x)) + (c,)
                pairs.append((index(y, x, c), index(*to)))
    return lax.ppermute(value, PLANE, pairs)


tied = lax.optimization_barrier


def wide(part):
    return part.astype(jnp.float32)


def reduce_start(partial):
    share = partial.shape[0] // 4
    half = share // 2
    up = ring(partial[share + half : 2 * share + half], "z", 1)
    down = ring(partial[2 * share + half : 3 * share + half], "z", -1)
    return up, down


def reduce_next(partial, up, down):
    share = partial.shape[0] // 4
    half = share // 2
    up_on = wide(partial[share : share + half]) + wide(up[half:])
    down_on = wide(partial[3 * share + half :]) + wide(down[:half])
    return (
        ring(up_on.astype(jnp.bfloat16), "z", 1),
        ring(down_on.astype(jnp.bfloat16), "z", -1),
    )


def reduce_end(partial, up, down, up_on, down_on):
    share = partial.shape[0] // 4
    half = share // 2
    return jnp.concatenate(
        [
            wide(partial[:half]) + wide(down[half:]) + wide(up_on),
            wide(partial[half:share]) + wide(up[:half]) + wide(down_on),
        ],
        axis=0,
    )


def spread_start(share):
    return ring(share, "z", 1), ring(share, "z", -1)


def spread_next(up, down):
    half = up.shape[0] // 2
    return ring(up[:half], "z", 1), ring(down[half:], "z", -1)


def spread_end(share, up, down, up_on, down_on):
    return jnp.concatenate([share, down, up_on, down_on, up], axis=0)


def by_share(pushed):
    return pushed.reshape(4, pushed.shape[0] // 4, pushed.shape[1])


def reduce_first(one, two):
    up = ring(jnp.concatenate([two[1], one[2]], axis=0), "z", 1)
    down = ring(jnp.concatenate([two[2], one[3]], axis=0), "z", -1)
    return up, down


def reduce_second(one, two, up, down):
    half = one.shape[1]
    up_on = (wide(one[1]) + wide(up[half:])).astype(jnp.bfloat16)
    down_on = (wide(two[3]) + wide(down[:half])).astype(jnp.bfloat16)
    return ring(up_on, "z", 1), ring(down_on, "z", -1)


def reduce_third(one, two, up, down, up_on, down_on):
    half = one.shape[1]
    return jnp.concatenate(
        [
            wide(one[0]) + wide(down[half:]) + wide(up_on),
            wide(two[0]) + wide(up[:half]) + wide(down_on),
        ],
        axis=0,
    )


def spread_first(share):
    return ring(share, "z", 1), ring(share, "z", -1)


def spread_second(up, down):
    half = up.shape[0] // 2
    return ring(up[:half], "z", 1), ring(down[half:], "z", -1)


def spread_third(share, up, down, up_on, down_on):
    half = share.shape[0] // 2
    return (
        jnp.concatenate([share[:half], down[:half], up_on, up[:half]], axis=0),
        jnp.concatenate([share[half:], down[half:], down_on, up[half:]], axis=0),
    )


def hop(value, axis, bits):
    return lax.ppermute(value, axis, [(i, i ^ bits) for i in range(4)])


def sum_ring(value, axis):
    return value + ring(value, axis, 1) + ring(value, axis, 2) + ring(value, axis, 3)


def first_half(own, gap_mine, gap_sent):
    y, xh, c, z, xl = (lax.axis_index(axis) for axis in AXES)
    x = 2 * xh + xl
    hops = jnp.array(HOPS, jnp.int32)

    def add(array, core, hop, before):
        first, second = hops, jnp.full((4,), hop, jnp.int32)
        at_x = x ^ jnp.where(core == 0, first, second)
        at_y = y ^ jnp.where(core == 0, second, first)
        share = jnp.where(core == 0, (at_y % 2) * 2 + at_x // 2, at_y)
        slot = jnp.zeros((4,), jnp.int32) + core
        column = jnp.where(at_x % 2 == xl, 0, 1).astype(jnp.int32)
        return unpack(array, (share + 4 - z) % 4, slot, column, before)

    line = jnp.concatenate([own] + [plane_step(own, 0, hop) for hop in HOPS[1:]], axis=0)
    near, past = plane_step(line, 1, 1), plane_step(line, 1, 3)
    other_line = swap(line, "c")
    one = [add(line, c, 0, [])]
    one = [add(other_line, 1 - c, 0, one)]

    near, past, one, gap_sent = tied((near, past, one, gap_sent))
    far = plane_step(near, 1, 3)
    gap_got = swap(gap_sent, "xl")
    other_near, other_past = swap(near, "c"), swap(past, "c")
    one = [add(near, c, 1, one)]
    one = add(other_near, 1 - c, 1, one)
    gap = jnp.concatenate([gap_mine, gap_got], axis=0)
    pushed_one = push(flat(one), gap)
    first_one = reduce_start(pushed_one)

    two = [add(past, c, 3, [])]
    two = [add(other_past, 1 - c, 3, two)]
    far, two, first_one = tied((far, two, first_one))
    other_far = swap(far, "c")
    next_one = reduce_next(pushed_one, *first_one)
    two = [add(far, c, 2, two)]
    two = add(other_far, 1 - c, 2, two)
    pushed_two = push(flat(two), gap)

    sign = jnp.where(jnp.arange(4 * TOK) < 2 * TOK, 1.0, -1.0)[:, None]

    def rounded(*parts):
        return (sign * reduce_end(*parts)).astype(jnp.bfloat16)

    pushed_two, next_one = tied((pushed_two, next_one))
    first_two = reduce_start(pushed_two)
    share_one = rounded(pushed_one, *first_one, *next_one)
    away_one = spread_start(share_one)
    first_two, away_one = tied((first_two, away_one))
    next_two = reduce_next(pushed_two, *first_two)
    on_one = spread_next(*away_one)
    next_two, on_one = tied((next_two, on_one))
    share_two = rounded(pushed_two, *first_two, *next_two)
    away_two = spread_start(share_two)
    start_one = pull_back(flat(one), spread_end(share_one, *away_one, *on_one))
    away_two, start_one = tied((away_two, start_one))
    on_two = spread_next(*away_two)
    start_two = pull_back(flat(two), spread_end(share_two, *away_two, *on_two))
    return flat(one), flat(two), start_one + start_two


def flat(chunk):
    return chunk.reshape(16 * TOK, 2 * HEADS * HD)


def pull_back(outputs, tangent):
    return lax.dot_general(
        outputs, tangent, (((0,), (0,)), ((), ())), preferred_element_type=jnp.float32
    )


def push(outputs, direction):
    return jnp.dot(outputs, direction, preferred_element_type=jnp.float32).astype(jnp.bfloat16)


def shards(queries_a, keys_a, values_a, queries_b, keys_b, values_b, out_a, out_b, lengths):
    xl = lax.axis_index("xl")
    token_total = 16 * TOK
    rows, width = out_a.shape[0], out_a.shape[1] // 2
    first = out_a.astype(jnp.float32)
    second = out_b.astype(jnp.float32)
    gap_low = ((first - second) * 0.5).astype(jnp.bfloat16)
    left, right = gap_low[:, :width], gap_low[:, width:]
    one, two, residual_start = first_half(
        attend(lengths, queries_a, keys_a, values_a, queries_b, keys_b, values_b),
        jnp.where(xl == 0, left, right),
        jnp.where(xl == 0, right, left),
    )
    residual_start = residual_start / token_total
    direction_low = residual_start.astype(jnp.bfloat16)

    pushed = by_share(push(one, direction_low)), by_share(push(two, direction_low))
    first = reduce_first(*pushed)
    other_start = swap(direction_low[rows:], "xl")
    residual_start, first = tied((residual_start, first))
    second = reduce_second(*pushed, *first)
    norm = jnp.sum(residual_start * residual_start, axis=0)
    norm, other_start, second = tied((norm, other_start, second))
    share = reduce_third(*pushed, *first, *second)
    low = share.astype(jnp.bfloat16)
    first = spread_first(low)
    totals = jnp.stack([norm, jnp.sum(share * share, axis=0)])
    totals = totals + swap(totals, "c")
    totals = totals + swap(totals, "xl")
    totals, first = tied((totals, first))
    second = spread_second(*first)
    totals = totals + swap(totals, "xh")
    totals, second = tied((totals, second))
    probe_one, probe_two = spread_third(low, *first, *second)
    image = pull_back(one, probe_one)
    totals = totals + hop(totals, "y", 1)
    totals, image = tied((totals, image))
    image = image + pull_back(two, probe_two)
    curvature = image / token_total + damping * residual_start
    sent = curvature[rows:].astype(jnp.bfloat16)
    sent, totals = tied((sent, totals))
    other_curvature = swap(sent, "xl")
    totals = totals + hop(totals, "y", 3)
    totals = jnp.stack([totals] + [ring(totals, "z", k) for k in (1, 2, 3)])
    totals, other_curvature = tied((totals, other_curvature))
    return finish(
        xl, totals, out_a, out_b, residual_start, curvature, other_start, other_curvature
    )


def solution(mesh):
    fine = Mesh(mesh.devices.reshape(4, 2, 2, 4, 2), AXES)
    dp, tensor = ("y", "xh", "c"), ("z", "xl")
    tokens = P(dp, tensor)
    return jax.shard_map(
        shards,
        mesh=fine,
        in_specs=(tokens,) * 6 + (P(tensor, dp),) * 2 + (P(dp, None),),
        out_specs=(P(tensor, dp), P(tensor, dp)),
        check_vma=False,
    )
```

```python
import math

import jax
import jax.numpy as jnp
from jax import lax
from jax.experimental import pallas as pl
from jax.experimental.pallas import tpu as pltpu
from jax.sharding import Mesh, PartitionSpec as P

HD = 128
HEADS = 8
TOK = 128
FOLD = 64
damping = 0.05
AXES = ("y", "xh", "c", "z", "xl")
PLANE = ("y", "xh", "c", "xl")
V_ROW = HEADS * TOK
END_ROW = V_ROW + 2 * TOK
ROWS = END_ROW + 16
HOPS = (0, 1, 3, 2)


def attend_kernel(lengths, qa, ka, va, qb, kb, vb, out):
    first = lengths[0, 0]
    second = first + lengths[0, 1]
    third = second + lengths[0, 2]

    def end_of(key):
        return jnp.where(
            key < first,
            first - 1,
            jnp.where(key < second, second - 1, jnp.where(key < third, third - 1, TOK - 1)),
        )

    key = lax.broadcasted_iota(jnp.int32, (TOK, TOK), 1)
    query = lax.broadcasted_iota(jnp.int32, (TOK, TOK), 0)
    allowed = (key <= query) & (query <= end_of(key))

    def folded(q_ref, k_ref, head):
        scores = lax.dot_general(
            q_ref[:, head * HD : (head + 1) * HD],
            k_ref[...],
            (((1,), (1,)), ((), ())),
            preferred_element_type=jnp.float32,
        ) / math.sqrt(HD)
        scores = jnp.where(allowed, scores, jnp.float32(-1e30))
        top = jnp.max(scores, axis=1, keepdims=True)
        exps = jnp.where(allowed, jnp.exp(scores - top), jnp.float32(0.0))
        weights = exps / jnp.sum(exps, axis=1, keepdims=True)
        return weights + pltpu.roll(weights, FOLD, 1)

    for head in range(HEADS):
        out[head * TOK : (head + 1) * TOK, :] = jnp.where(
            key < FOLD, folded(qa, ka, head), folded(qb, kb, head)
        ).astype(jnp.bfloat16)
    out[V_ROW : V_ROW + TOK, :] = va[...]
    out[V_ROW + TOK : END_ROW, :] = vb[...]
    lane = lax.broadcasted_iota(jnp.int32, (16, TOK), 1) & (FOLD - 1)
    row = lax.broadcasted_iota(jnp.int32, (16, TOK), 0)
    ends = end_of(jnp.where(row < 8, lane, lane + FOLD))
    out[END_ROW:, :] = ends.astype(jnp.float32).astype(jnp.bfloat16)


def attend(lengths, *operands):
    def whole(shape):
        return pl.BlockSpec(shape, lambda i: (0, 0))

    return pl.pallas_call(
        attend_kernel,
        out_shape=jax.ShapeDtypeStruct((ROWS, TOK), jnp.bfloat16),
        grid=(1,),
        in_specs=[pl.BlockSpec(memory_space=pltpu.SMEM)] + [whole(o.shape) for o in operands],
        out_specs=whole((ROWS, TOK)),
        compiler_params=pltpu.CompilerParams(vmem_limit_bytes=60 << 20),
        cost_estimate=pl.CostEstimate(flops=1, bytes_accessed=1, transcendentals=0),
    )(lengths, *operands)


def unpack_kernel(place, slot, column, block, *refs):
    out = refs[-1]
    ends = block[END_ROW:, :].astype(jnp.float32)
    end_low, end_high = ends[0:1, :].astype(jnp.int32), ends[8:9, :].astype(jnp.int32)
    key = lax.broadcasted_iota(jnp.int32, (TOK, TOK), 1) & (FOLD - 1)
    query = lax.broadcasted_iota(jnp.int32, (TOK, TOK), 0)
    low = jnp.where((key <= query) & (query <= end_low), 1.0, 0.0).astype(jnp.bfloat16)
    high = jnp.where((key + FOLD <= query) & (query <= end_high), 1.0, 0.0).astype(jnp.bfloat16)
    packed = block[:V_ROW, :].reshape(HEADS, TOK, TOK)
    weights = jnp.concatenate(
        [(packed * low[None]).reshape(V_ROW, TOK), (packed * high[None]).reshape(V_ROW, TOK)], axis=1
    )
    va, vb = block[V_ROW : V_ROW + TOK, :], block[V_ROW + TOK : END_ROW, :]
    none = jnp.zeros((FOLD, HD), jnp.bfloat16)
    values = jnp.concatenate(
        [
            jnp.concatenate([va[:FOLD], none], axis=1),
            jnp.concatenate([none, vb[:FOLD]], axis=1),
            jnp.concatenate([va[FOLD:], none], axis=1),
            jnp.concatenate([none, vb[FOLD:]], axis=1),
        ],
        axis=0,
    )
    mixed = jnp.dot(weights, values, preferred_element_type=jnp.float32).astype(jnp.bfloat16)
    for head in range(HEADS):
        part = mixed[head * TOK : (head + 1) * TOK, :]
        out[0, 0, 0, :, head * HD : (head + 1) * HD] = part[:, :HD]
        out[0, 1, 0, :, head * HD : (head + 1) * HD] = part[:, HD:]


def unpack(blocks, place, slot, column, before):
    count = blocks.shape[0] // ROWS
    return pl.pallas_call(
        unpack_kernel,
        out_shape=jax.ShapeDtypeStruct((4, 2, 2, TOK, 2 * HEADS * HD), jnp.bfloat16),
        grid_spec=pltpu.PrefetchScalarGridSpec(
            num_scalar_prefetch=3,
            grid=(count,),
            in_specs=[pl.BlockSpec((ROWS, TOK), lambda i, p, s, c: (i, 0))]
            + [pl.BlockSpec(memory_space=pl.ANY)] * len(before),
            out_specs=pl.BlockSpec(
                (1, 2, 1, TOK, HEADS * HD), lambda i, p, s, c: (p[i], 0, s[i], 0, c[i])
            ),
        ),
        input_output_aliases={4: 0} if before else {},
        compiler_params=pltpu.CompilerParams(vmem_limit_bytes=16 << 20),
        cost_estimate=pl.CostEstimate(flops=1, bytes_accessed=1, transcendentals=0),
    )(place, slot, column, blocks, *before)


def finish_kernel(
    column, sums, out_a, out_b, start, curvature, other_start, other_curvature, merged, residual
):
    norm = jnp.sum(sums[:, 0, :])
    step = norm / (jnp.sum(sums[:, 1, :]) / (16 * TOK) + damping * norm)
    midpoint = (out_a[...].astype(jnp.float32) + out_b[...].astype(jnp.float32)) * 0.5

    def write(begin, image):
        merged[...] = midpoint + step * begin
        residual[...] = begin - step * image

    @pl.when(pl.program_id(0) == 0)
    def _():
        write(start[...], curvature[...])

    @pl.when(pl.program_id(0) == 1)
    def _():
        write(other_start[...].astype(jnp.float32), other_curvature[...].astype(jnp.float32))


def finish(xl, sums, out_a, out_b, start, curvature, other_start, other_curvature):
    rows, width = other_start.shape
    tile = rows
    placed = pl.BlockSpec((tile, width), lambda i, r, x: (r, (i + x[0]) % 2))
    mine = pl.BlockSpec((tile, width), lambda i, r, x: (r, 0))
    other = pl.BlockSpec((tile, width), lambda i, r, x: (r, 0))
    shape = jax.ShapeDtypeStruct((rows, 2 * width), jnp.float32)
    return pl.pallas_call(
        finish_kernel,
        out_shape=[shape, shape],
        grid_spec=pltpu.PrefetchScalarGridSpec(
            num_scalar_prefetch=1,
            grid=(2, 1),
            in_specs=[pl.BlockSpec(sums.shape, lambda i, r, x: (0, 0, 0)), placed, placed, mine, mine, other, other],
            out_specs=[placed, placed],
        ),
        compiler_params=pltpu.CompilerParams(vmem_limit_bytes=56 << 20),
        cost_estimate=pl.CostEstimate(flops=1, bytes_accessed=1, transcendentals=0),
    )(
        xl.reshape(1),
        sums,
        out_a,
        out_b,
        start,
        curvature,
        other_start,
        other_curvature,
    )


def ring(value, axis, shift):
    return lax.ppermute(value, axis, [(i, (i + shift) % 4) for i in range(4)])


def swap(value, axis):
    return lax.ppermute(value, axis, [(0, 1), (1, 0)])


def plane_step(value, stage, hop):
    def index(y, x, c):
        return ((y * 2 + x // 2) * 2 + c) * 2 + x % 2

    pairs = []
    for y in range(4):
        for x in range(4):
            for c in range(2):
                along_x = (stage + c) % 2 == 0
                to = ((y, x ^ hop) if along_x else (y ^ hop, x)) + (c,)
                pairs.append((index(y, x, c), index(*to)))
    return lax.ppermute(value, PLANE, pairs)


tied = lax.optimization_barrier


def wide(part):
    return part.astype(jnp.float32)


def reduce_parts(partial):
    share = partial.shape[0] // 4
    half = share // 2
    return partial[share + half : 2 * share + half], partial[2 * share + half : 3 * share + half]


def reduce_start(partial):
    up, down = reduce_parts(partial)
    return ring(up, "z", 1), ring(down, "z", -1)


def reduce_next_parts(partial, up, down):
    share = partial.shape[0] // 4
    half = share // 2
    up_on = wide(partial[share : share + half]) + wide(up[half:])
    down_on = wide(partial[3 * share + half :]) + wide(down[:half])
    return up_on.astype(jnp.bfloat16), down_on.astype(jnp.bfloat16)


def reduce_next(partial, up, down):
    up_on, down_on = reduce_next_parts(partial, up, down)
    return ring(up_on, "z", 1), ring(down_on, "z", -1)


def reduce_end(partial, up, down, up_on, down_on):
    share = partial.shape[0] // 4
    half = share // 2
    return jnp.concatenate(
        [
            wide(partial[:half]) + wide(down[half:]) + wide(up_on),
            wide(partial[half:share]) + wide(up[:half]) + wide(down_on),
        ],
        axis=0,
    )


def spread_start(share):
    return ring(share, "z", 1), ring(share, "z", -1)


def spread_next(up, down):
    half = up.shape[0] // 2
    return ring(up[:half], "z", 1), ring(down[half:], "z", -1)


def spread_end(share, up, down, up_on, down_on):
    return jnp.concatenate([share, down, up_on, down_on, up], axis=0)


def by_share(pushed):
    return pushed.reshape(4, pushed.shape[0] // 4, pushed.shape[1])


def reduce_first(one, two):
    up = ring(jnp.concatenate([two[1], one[2]], axis=0), "z", 1)
    down = ring(jnp.concatenate([two[2], one[3]], axis=0), "z", -1)
    return up, down


def reduce_second(one, two, up, down):
    half = one.shape[1]
    up_on = (wide(one[1]) + wide(up[half:])).astype(jnp.bfloat16)
    down_on = (wide(two[3]) + wide(down[:half])).astype(jnp.bfloat16)
    return ring(up_on, "z", 1), ring(down_on, "z", -1)


def reduce_third(one, two, up, down, up_on, down_on):
    half = one.shape[1]
    return jnp.concatenate(
        [
            wide(one[0]) + wide(down[half:]) + wide(up_on),
            wide(two[0]) + wide(up[:half]) + wide(down_on),
        ],
        axis=0,
    )


def spread_first(share):
    return ring(share, "z", 1), ring(share, "z", -1)


def spread_second(up, down):
    half = up.shape[0] // 2
    return ring(up[:half], "z", 1), ring(down[half:], "z", -1)


def spread_third(share, up, down, up_on, down_on):
    half = share.shape[0] // 2
    return (
        jnp.concatenate([share[:half], down[:half], up_on, up[:half]], axis=0),
        jnp.concatenate([share[half:], down[half:], down_on, up[half:]], axis=0),
    )


def hop(value, axis, bits):
    return lax.ppermute(value, axis, [(i, i ^ bits) for i in range(4)])


def sum_ring(value, axis):
    return value + ring(value, axis, 1) + ring(value, axis, 2) + ring(value, axis, 3)


def first_half(own, gap_mine, gap_sent):
    y, xh, c, z, xl = (lax.axis_index(axis) for axis in AXES)
    x = 2 * xh + xl
    hops = jnp.array(HOPS, jnp.int32)

    def add(array, core, hop, before):
        first, second = hops, jnp.full((4,), hop, jnp.int32)
        at_x = x ^ jnp.where(core == 0, first, second)
        at_y = y ^ jnp.where(core == 0, second, first)
        share = jnp.where(core == 0, (at_y % 2) * 2 + at_x // 2, at_y)
        slot = jnp.zeros((4,), jnp.int32) + core
        column = jnp.where(at_x % 2 == xl, 0, 1).astype(jnp.int32)
        return unpack(array, (share + 4 - z) % 4, slot, column, before)

    line = jnp.concatenate([own] + [plane_step(own, 0, hop) for hop in HOPS[1:]], axis=0)
    near, past = plane_step(line, 1, 1), plane_step(line, 1, 3)
    other_line = swap(line, "c")
    one = [add(line, c, 0, [])]
    one = [add(other_line, 1 - c, 0, one)]

    near, past, one, gap_sent = tied((near, past, one, gap_sent))
    far = plane_step(near, 1, 3)
    gap_got = swap(gap_sent, "xl")
    other_near, other_past = swap(near, "c"), swap(past, "c")
    one = [add(near, c, 1, one)]
    one = add(other_near, 1 - c, 1, one)
    two = [add(past, c, 3, [])]
    two = add(other_past, 1 - c, 3, two)
    gap_got, one, two = tied((gap_got, one, two))
    gap = jnp.concatenate([gap_mine, gap_got], axis=0)
    pushed_one = push(flat(one), gap)
    far, two, pushed_one = tied((far, two, pushed_one))
    first_one = reduce_start(pushed_one)
    other_far = swap(far, "c")
    two = add(far, c, 2, [two])
    two, other_far, first_one = tied((two, other_far, first_one))
    next_one = reduce_next(pushed_one, *first_one)
    two = add(other_far, 1 - c, 2, [two])
    pushed_two = push(flat(two), gap)

    sign = jnp.where(jnp.arange(4 * TOK) < 2 * TOK, 1.0, -1.0)[:, None]

    def rounded(*parts):
        return (sign * reduce_end(*parts)).astype(jnp.bfloat16)

    def both_ways(first, second):
        cut = first[0].shape[0]
        up = ring(jnp.concatenate([first[0], second[0]], axis=0), "z", 1)
        down = ring(jnp.concatenate([first[1], second[1]], axis=0), "z", -1)
        up, down = tied((up, down))
        return (up[:cut], down[:cut]), (up[cut:], down[cut:])

    pushed_two, next_one = tied((pushed_two, next_one))
    share_one = rounded(pushed_one, *first_one, *next_one)
    first_two, away_one = both_ways(reduce_parts(pushed_two), (share_one, share_one))
    half = share_one.shape[0] // 2
    next_two, on_one = both_ways(
        reduce_next_parts(pushed_two, *first_two), (away_one[0][:half], away_one[1][half:])
    )
    share_two = rounded(pushed_two, *first_two, *next_two)
    away_two = spread_start(share_two)
    start_one = pull_back(flat(one), spread_end(share_one, *away_one, *on_one))
    away_two, start_one = tied((away_two, start_one))
    on_two = spread_next(*away_two)
    start_two = pull_back(flat(two), spread_end(share_two, *away_two, *on_two))
    return flat(one), flat(two), start_one + start_two


def flat(chunk):
    return chunk.reshape(16 * TOK, 2 * HEADS * HD)


def pull_back(outputs, tangent):
    return lax.dot_general(
        outputs, tangent, (((0,), (0,)), ((), ())), preferred_element_type=jnp.float32
    )


def push(outputs, direction):
    return jnp.dot(outputs, direction, preferred_element_type=jnp.float32).astype(jnp.bfloat16)


def shards(queries_a, keys_a, values_a, queries_b, keys_b, values_b, out_a, out_b, lengths):
    xl = lax.axis_index("xl")
    token_total = 16 * TOK
    rows, width = out_a.shape[0], out_a.shape[1] // 2
    first = out_a.astype(jnp.float32)
    second = out_b.astype(jnp.float32)
    gap_low = ((first - second) * 0.5).astype(jnp.bfloat16)
    left, right = gap_low[:, :width], gap_low[:, width:]
    one, two, residual_start = first_half(
        attend(lengths, queries_a, keys_a, values_a, queries_b, keys_b, values_b),
        jnp.where(xl == 0, left, right),
        jnp.where(xl == 0, right, left),
    )
    residual_start = residual_start / token_total
    direction_low = residual_start.astype(jnp.bfloat16)

    pushed = by_share(push(one, direction_low)), by_share(push(two, direction_low))
    first = reduce_first(*pushed)
    other_start = swap(direction_low[rows:], "xl")
    residual_start, first = tied((residual_start, first))
    second = reduce_second(*pushed, *first)
    norm = jnp.sum(residual_start * residual_start, axis=0)
    norm, other_start, second = tied((norm, other_start, second))
    share = reduce_third(*pushed, *first, *second)
    low = share.astype(jnp.bfloat16)
    first = spread_first(low)
    totals = jnp.stack([norm, jnp.sum(share * share, axis=0)])
    totals = totals + swap(totals, "c")
    totals = totals + swap(totals, "xl")
    totals, first = tied((totals, first))
    second = spread_second(*first)
    totals = totals + swap(totals, "xh")
    totals, second = tied((totals, second))
    probe_one, probe_two = spread_third(low, *first, *second)
    image = pull_back(one, probe_one)
    totals = totals + hop(totals, "y", 1)
    totals, image = tied((totals, image))
    image = image + pull_back(two, probe_two)
    curvature = image / token_total + damping * residual_start
    sent = curvature[rows:].astype(jnp.bfloat16)
    sent, totals = tied((sent, totals))
    other_curvature = swap(sent, "xl")
    totals = totals + hop(totals, "y", 3)
    totals = jnp.stack([totals] + [ring(totals, "z", k) for k in (1, 2, 3)])
    totals, other_curvature = tied((totals, other_curvature))
    return finish(
        xl, totals, out_a, out_b, residual_start, curvature, other_start, other_curvature
    )


def solution(mesh):
    fine = Mesh(mesh.devices.reshape(4, 2, 2, 4, 2), AXES)
    dp, tensor = ("y", "xh", "c"), ("z", "xl")
    tokens = P(dp, tensor)
    return jax.shard_map(
        shards,
        mesh=fine,
        in_specs=(tokens,) * 6 + (P(tensor, dp),) * 2 + (P(dp, None),),
        out_specs=(P(tensor, dp), P(tensor, dp)),
        check_vma=False,
    )
```

```python
import math

import jax
import jax.numpy as jnp
from jax import lax
from jax.experimental import pallas as pl
from jax.experimental.pallas import tpu as pltpu
from jax.sharding import Mesh, PartitionSpec as P

HD = 128
HEADS = 8
TOK = 128
FOLD = 64
damping = 0.05
AXES = ("y", "xh", "c", "z", "xl")
PLANE = ("y", "xh", "c", "xl")
V_ROW = HEADS * TOK
END_ROW = V_ROW + 2 * TOK
ROWS = END_ROW + 16
HOPS = (0, 1, 3, 2)


def attend_kernel(lengths, qa, ka, va, qb, kb, vb, out):
    first = lengths[0, 0]
    second = first + lengths[0, 1]
    third = second + lengths[0, 2]

    def end_of(key):
        return jnp.where(
            key < first,
            first - 1,
            jnp.where(key < second, second - 1, jnp.where(key < third, third - 1, TOK - 1)),
        )

    key = lax.broadcasted_iota(jnp.int32, (TOK, TOK), 1)
    query = lax.broadcasted_iota(jnp.int32, (TOK, TOK), 0)
    allowed = (key <= query) & (query <= end_of(key))

    def folded(q_ref, k_ref, head):
        scores = lax.dot_general(
            q_ref[:, head * HD : (head + 1) * HD],
            k_ref[...],
            (((1,), (1,)), ((), ())),
            preferred_element_type=jnp.float32,
        ) / math.sqrt(HD)
        scores = jnp.where(allowed, scores, jnp.float32(-1e30))
        top = jnp.max(scores, axis=1, keepdims=True)
        exps = jnp.where(allowed, jnp.exp(scores - top), jnp.float32(0.0))
        weights = exps / jnp.sum(exps, axis=1, keepdims=True)
        return weights + pltpu.roll(weights, FOLD, 1)

    for head in range(HEADS):
        out[head * TOK : (head + 1) * TOK, :] = jnp.where(
            key < FOLD, folded(qa, ka, head), folded(qb, kb, head)
        ).astype(jnp.bfloat16)
    out[V_ROW : V_ROW + TOK, :] = va[...]
    out[V_ROW + TOK : END_ROW, :] = vb[...]
    lane = lax.broadcasted_iota(jnp.int32, (16, TOK), 1) & (FOLD - 1)
    row = lax.broadcasted_iota(jnp.int32, (16, TOK), 0)
    ends = end_of(jnp.where(row < 8, lane, lane + FOLD))
    out[END_ROW:, :] = ends.astype(jnp.float32).astype(jnp.bfloat16)


def attend(lengths, *operands):
    def whole(shape):
        return pl.BlockSpec(shape, lambda i: (0, 0))

    return pl.pallas_call(
        attend_kernel,
        out_shape=jax.ShapeDtypeStruct((ROWS, TOK), jnp.bfloat16),
        grid=(1,),
        in_specs=[pl.BlockSpec(memory_space=pltpu.SMEM)] + [whole(o.shape) for o in operands],
        out_specs=whole((ROWS, TOK)),
        compiler_params=pltpu.CompilerParams(vmem_limit_bytes=60 << 20),
        cost_estimate=pl.CostEstimate(flops=1, bytes_accessed=1, transcendentals=0),
    )(lengths, *operands)


def unpack_kernel(place, slot, column, block, *refs):
    out = refs[-1]
    ends = block[END_ROW:, :].astype(jnp.float32)
    end_low, end_high = ends[0:1, :].astype(jnp.int32), ends[8:9, :].astype(jnp.int32)
    key = lax.broadcasted_iota(jnp.int32, (TOK, TOK), 1) & (FOLD - 1)
    query = lax.broadcasted_iota(jnp.int32, (TOK, TOK), 0)
    low = jnp.where((key <= query) & (query <= end_low), 1.0, 0.0).astype(jnp.bfloat16)
    high = jnp.where((key + FOLD <= query) & (query <= end_high), 1.0, 0.0).astype(jnp.bfloat16)
    packed = block[:V_ROW, :].reshape(HEADS, TOK, TOK)
    weights = jnp.concatenate(
        [(packed * low[None]).reshape(V_ROW, TOK), (packed * high[None]).reshape(V_ROW, TOK)], axis=1
    )
    va, vb = block[V_ROW : V_ROW + TOK, :], block[V_ROW + TOK : END_ROW, :]
    none = jnp.zeros((FOLD, HD), jnp.bfloat16)
    values = jnp.concatenate(
        [
            jnp.concatenate([va[:FOLD], none], axis=1),
            jnp.concatenate([none, vb[:FOLD]], axis=1),
            jnp.concatenate([va[FOLD:], none], axis=1),
            jnp.concatenate([none, vb[FOLD:]], axis=1),
        ],
        axis=0,
    )
    mixed = jnp.dot(weights, values, preferred_element_type=jnp.float32).astype(jnp.bfloat16)
    for head in range(HEADS):
        part = mixed[head * TOK : (head + 1) * TOK, :]
        out[0, 0, 0, :, head * HD : (head + 1) * HD] = part[:, :HD]
        out[0, 1, 0, :, head * HD : (head + 1) * HD] = part[:, HD:]


def unpack(blocks, place, slot, column, before):
    count = blocks.shape[0] // ROWS
    return pl.pallas_call(
        unpack_kernel,
        out_shape=jax.ShapeDtypeStruct((4, 2, 2, TOK, 2 * HEADS * HD), jnp.bfloat16),
        grid_spec=pltpu.PrefetchScalarGridSpec(
            num_scalar_prefetch=3,
            grid=(count,),
            in_specs=[pl.BlockSpec((ROWS, TOK), lambda i, p, s, c: (i, 0))]
            + [pl.BlockSpec(memory_space=pl.ANY)] * len(before),
            out_specs=pl.BlockSpec(
                (1, 2, 1, TOK, HEADS * HD), lambda i, p, s, c: (p[i], 0, s[i], 0, c[i])
            ),
        ),
        input_output_aliases={4: 0} if before else {},
        compiler_params=pltpu.CompilerParams(vmem_limit_bytes=16 << 20),
        cost_estimate=pl.CostEstimate(flops=1, bytes_accessed=1, transcendentals=0),
    )(place, slot, column, blocks, *before)


def finish_kernel(
    column, sums, out_a, out_b, start, curvature, other_start, other_curvature, merged, residual
):
    norm = jnp.sum(sums[:, 0, :])
    step = norm / (jnp.sum(sums[:, 1, :]) / (16 * TOK) + damping * norm)
    midpoint = (out_a[...].astype(jnp.float32) + out_b[...].astype(jnp.float32)) * 0.5

    def write(begin, image):
        merged[...] = midpoint + step * begin
        residual[...] = begin - step * image

    @pl.when(pl.program_id(0) == 0)
    def _():
        write(start[...], curvature[...])

    @pl.when(pl.program_id(0) == 1)
    def _():
        write(other_start[...].astype(jnp.float32), other_curvature[...].astype(jnp.float32))


def finish(xl, sums, out_a, out_b, start, curvature, other_start, other_curvature):
    rows, width = other_start.shape
    tile = rows
    placed = pl.BlockSpec((tile, width), lambda i, r, x: (r, (i + x[0]) % 2))
    mine = pl.BlockSpec((tile, width), lambda i, r, x: (r, 0))
    other = pl.BlockSpec((tile, width), lambda i, r, x: (r, 0))
    shape = jax.ShapeDtypeStruct((rows, 2 * width), jnp.float32)
    return pl.pallas_call(
        finish_kernel,
        out_shape=[shape, shape],
        grid_spec=pltpu.PrefetchScalarGridSpec(
            num_scalar_prefetch=1,
            grid=(2, 1),
            in_specs=[pl.BlockSpec(sums.shape, lambda i, r, x: (0, 0, 0)), placed, placed, mine, mine, other, other],
            out_specs=[placed, placed],
        ),
        compiler_params=pltpu.CompilerParams(vmem_limit_bytes=56 << 20),
        cost_estimate=pl.CostEstimate(flops=1, bytes_accessed=1, transcendentals=0),
    )(
        xl.reshape(1),
        sums,
        out_a,
        out_b,
        start,
        curvature,
        other_start,
        other_curvature,
    )


def ring(value, axis, shift):
    return lax.ppermute(value, axis, [(i, (i + shift) % 4) for i in range(4)])


def swap(value, axis):
    return lax.ppermute(value, axis, [(0, 1), (1, 0)])


def plane_step(value, stage, hop):
    def index(y, x, c):
        return ((y * 2 + x // 2) * 2 + c) * 2 + x % 2

    pairs = []
    for y in range(4):
        for x in range(4):
            for c in range(2):
                along_x = (stage + c) % 2 == 0
                to = ((y, x ^ hop) if along_x else (y ^ hop, x)) + (c,)
                pairs.append((index(y, x, c), index(*to)))
    return lax.ppermute(value, PLANE, pairs)


tied = lax.optimization_barrier


def wide(part):
    return part.astype(jnp.float32)


def reduce_parts(partial):
    share = partial.shape[0] // 4
    half = share // 2
    return partial[share + half : 2 * share + half], partial[2 * share + half : 3 * share + half]


def reduce_start(partial):
    up, down = reduce_parts(partial)
    return ring(up, "z", 1), ring(down, "z", -1)


def reduce_next_parts(partial, up, down):
    share = partial.shape[0] // 4
    half = share // 2
    up_on = wide(partial[share : share + half]) + wide(up[half:])
    down_on = wide(partial[3 * share + half :]) + wide(down[:half])
    return up_on.astype(jnp.bfloat16), down_on.astype(jnp.bfloat16)


def reduce_next(partial, up, down):
    up_on, down_on = reduce_next_parts(partial, up, down)
    return ring(up_on, "z", 1), ring(down_on, "z", -1)


def reduce_end(partial, up, down, up_on, down_on):
    share = partial.shape[0] // 4
    half = share // 2
    return jnp.concatenate(
        [
            wide(partial[:half]) + wide(down[half:]) + wide(up_on),
            wide(partial[half:share]) + wide(up[:half]) + wide(down_on),
        ],
        axis=0,
    )


def spread_start(share):
    return ring(share, "z", 1), ring(share, "z", -1)


def spread_next(up, down):
    half = up.shape[0] // 2
    return ring(up[:half], "z", 1), ring(down[half:], "z", -1)


def spread_end(share, up, down, up_on, down_on):
    return jnp.concatenate([share, down, up_on, down_on, up], axis=0)


def by_share(pushed):
    return pushed.reshape(4, pushed.shape[0] // 4, pushed.shape[1])


def reduce_first(one, two):
    up = ring(jnp.concatenate([two[1], one[2]], axis=0), "z", 1)
    down = ring(jnp.concatenate([two[2], one[3]], axis=0), "z", -1)
    return up, down


def reduce_second(one, two, up, down):
    half = one.shape[1]
    up_on = (wide(one[1]) + wide(up[half:])).astype(jnp.bfloat16)
    down_on = (wide(two[3]) + wide(down[:half])).astype(jnp.bfloat16)
    return ring(up_on, "z", 1), ring(down_on, "z", -1)


def reduce_third(one, two, up, down, up_on, down_on):
    half = one.shape[1]
    return jnp.concatenate(
        [
            wide(one[0]) + wide(down[half:]) + wide(up_on),
            wide(two[0]) + wide(up[:half]) + wide(down_on),
        ],
        axis=0,
    )


def spread_first(share):
    return ring(share, "z", 1), ring(share, "z", -1)


def spread_second(up, down):
    half = up.shape[0] // 2
    return ring(up[:half], "z", 1), ring(down[half:], "z", -1)


def spread_third(share, up, down, up_on, down_on):
    half = share.shape[0] // 2
    return (
        jnp.concatenate([share[:half], down[:half], up_on, up[:half]], axis=0),
        jnp.concatenate([share[half:], down[half:], down_on, up[half:]], axis=0),
    )


def first_half(own, gap_mine, gap_sent):
    y, xh, c, z, xl = (lax.axis_index(axis) for axis in AXES)
    x = 2 * xh + xl
    hops = jnp.array(HOPS, jnp.int32)

    def add(array, core, hop, before):
        first, second = hops, jnp.full((4,), hop, jnp.int32)
        at_x = x ^ jnp.where(core == 0, first, second)
        at_y = y ^ jnp.where(core == 0, second, first)
        share = jnp.where(core == 0, (at_y % 2) * 2 + at_x // 2, at_y)
        slot = jnp.zeros((4,), jnp.int32) + core
        column = jnp.where(at_x % 2 == xl, 0, 1).astype(jnp.int32)
        return unpack(array, (share + 4 - z) % 4, slot, column, before)

    line = jnp.concatenate([own] + [plane_step(own, 0, hop) for hop in HOPS[1:]], axis=0)
    near, past = plane_step(line, 1, 1), plane_step(line, 1, 3)
    other_line = swap(line, "c")
    one = [add(line, c, 0, [])]
    one = [add(other_line, 1 - c, 0, one)]

    near, past, one, gap_sent = tied((near, past, one, gap_sent))
    far = plane_step(near, 1, 3)
    gap_got = swap(gap_sent, "xl")
    other_near, other_past = swap(near, "c"), swap(past, "c")
    one = [add(near, c, 1, one)]
    one = add(other_near, 1 - c, 1, one)
    two = [add(past, c, 3, [])]
    two = add(other_past, 1 - c, 3, two)
    gap_got, one, two = tied((gap_got, one, two))
    gap = jnp.concatenate([gap_mine, gap_got], axis=0)
    pushed_one = push(flat(one), gap)
    far, two, pushed_one = tied((far, two, pushed_one))
    first_one = reduce_start(pushed_one)
    other_far = swap(far, "c")
    two = add(far, c, 2, [two])
    two, other_far, first_one = tied((two, other_far, first_one))
    next_one = reduce_next(pushed_one, *first_one)
    two = add(other_far, 1 - c, 2, [two])
    pushed_two = push(flat(two), gap)

    sign = jnp.where(jnp.arange(4 * TOK) < 2 * TOK, 1.0, -1.0)[:, None]

    def rounded(*parts):
        return (sign * reduce_end(*parts)).astype(jnp.bfloat16)

    def both_ways(first, second):
        cut = first[0].shape[0]
        up = ring(jnp.concatenate([first[0], second[0]], axis=0), "z", 1)
        down = ring(jnp.concatenate([first[1], second[1]], axis=0), "z", -1)
        up, down = tied((up, down))
        return (up[:cut], down[:cut]), (up[cut:], down[cut:])

    pushed_two, next_one = tied((pushed_two, next_one))
    share_one = rounded(pushed_one, *first_one, *next_one)
    first_two, away_one = both_ways(reduce_parts(pushed_two), (share_one, share_one))
    half = share_one.shape[0] // 2
    next_two, on_one = both_ways(
        reduce_next_parts(pushed_two, *first_two), (away_one[0][:half], away_one[1][half:])
    )
    share_two = rounded(pushed_two, *first_two, *next_two)
    away_two = spread_start(share_two)
    start_one = pull_back(flat(one), spread_end(share_one, *away_one, *on_one))
    away_two, start_one = tied((away_two, start_one))
    on_two = spread_next(*away_two)
    start_two = pull_back(flat(two), spread_end(share_two, *away_two, *on_two))
    return flat(one), flat(two), start_one + start_two


def flat(chunk):
    return chunk.reshape(16 * TOK, 2 * HEADS * HD)


def pull_back(outputs, tangent):
    return lax.dot_general(
        outputs, tangent, (((0,), (0,)), ((), ())), preferred_element_type=jnp.float32
    )


def push(outputs, direction):
    return jnp.dot(outputs, direction, preferred_element_type=jnp.float32).astype(jnp.bfloat16)


def shards(queries_a, keys_a, values_a, queries_b, keys_b, values_b, out_a, out_b, lengths):
    xl = lax.axis_index("xl")
    token_total = 16 * TOK
    rows, width = out_a.shape[0], out_a.shape[1] // 2
    first = out_a.astype(jnp.float32)
    second = out_b.astype(jnp.float32)
    gap_low = ((first - second) * 0.5).astype(jnp.bfloat16)
    left, right = gap_low[:, :width], gap_low[:, width:]
    one, two, residual_start = first_half(
        attend(lengths, queries_a, keys_a, values_a, queries_b, keys_b, values_b),
        jnp.where(xl == 0, left, right),
        jnp.where(xl == 0, right, left),
    )
    residual_start = residual_start / token_total
    direction_low = residual_start.astype(jnp.bfloat16)

    pushed = by_share(push(one, direction_low)), by_share(push(two, direction_low))
    first = reduce_first(*pushed)
    other_start = swap(direction_low[rows:], "xl")
    residual_start, first = tied((residual_start, first))
    second = reduce_second(*pushed, *first)
    norm = jnp.sum(residual_start * residual_start, axis=0)
    norm, other_start, second = tied((norm, other_start, second))
    share = reduce_third(*pushed, *first, *second)
    low = share.astype(jnp.bfloat16)
    first = spread_first(low)
    totals = jnp.stack([norm, jnp.sum(share * share, axis=0)])
    totals = totals + swap(totals, "c")
    totals = totals + plane_step(totals, 0, 1)
    totals, first = tied((totals, first))
    second = spread_second(*first)
    totals = totals + plane_step(totals, 0, 3)
    totals, second = tied((totals, second))
    probe_one, probe_two = spread_third(low, *first, *second)
    image = pull_back(one, probe_one)
    totals = totals + plane_step(totals, 1, 1)
    totals, image = tied((totals, image))
    image = image + pull_back(two, probe_two)
    curvature = image / token_total + damping * residual_start
    sent = curvature[rows:].astype(jnp.bfloat16)
    other_curvature = swap(sent, "xl")
    totals = totals + plane_step(totals, 1, 3)
    totals = jnp.stack([totals] + [ring(totals, "z", k) for k in (1, 2, 3)])
    totals, other_curvature = tied((totals, other_curvature))
    return finish(
        xl, totals, out_a, out_b, residual_start, curvature, other_start, other_curvature
    )


def solution(mesh):
    fine = Mesh(mesh.devices.reshape(4, 2, 2, 4, 2), AXES)
    dp, tensor = ("y", "xh", "c"), ("z", "xl")
    tokens = P(dp, tensor)
    return jax.shard_map(
        shards,
        mesh=fine,
        in_specs=(tokens,) * 6 + (P(tensor, dp),) * 2 + (P(dp, None),),
        out_specs=(P(tensor, dp), P(tensor, dp)),
        check_vma=False,
    )
```

```python
import math

import jax
import jax.numpy as jnp
from jax import lax
from jax.experimental import pallas as pl
from jax.experimental.pallas import tpu as pltpu
from jax.sharding import Mesh, PartitionSpec as P

HD = 128
HEADS = 8
TOK = 128
FOLD = 64
damping = 0.05
AXES = ("y", "xh", "c", "z", "xl")
PLANE = ("y", "xh", "c", "xl")
V_ROW = HEADS * TOK
END_ROW = V_ROW + 2 * TOK
ROWS = END_ROW + 16
HOPS = (0, 1, 3, 2)


def attend_kernel(lengths, qa, ka, va, qb, kb, vb, out):
    first = lengths[0, 0]
    second = first + lengths[0, 1]
    third = second + lengths[0, 2]

    def end_of(key):
        return jnp.where(
            key < first,
            first - 1,
            jnp.where(key < second, second - 1, jnp.where(key < third, third - 1, TOK - 1)),
        )

    key = lax.broadcasted_iota(jnp.int32, (TOK, TOK), 1)
    query = lax.broadcasted_iota(jnp.int32, (TOK, TOK), 0)
    allowed = (key <= query) & (query <= end_of(key))

    def folded(q_ref, k_ref, head):
        scores = lax.dot_general(
            q_ref[:, head * HD : (head + 1) * HD],
            k_ref[...],
            (((1,), (1,)), ((), ())),
            preferred_element_type=jnp.float32,
        ) * (1.0 / math.sqrt(HD))
        scores = jnp.where(allowed, scores, jnp.float32(-1e30))
        top = jnp.max(scores, axis=1, keepdims=True)
        exps = jnp.where(allowed, jnp.exp(scores - top), jnp.float32(0.0))
        weights = exps * (1.0 / jnp.sum(exps, axis=1, keepdims=True))
        return weights + pltpu.roll(weights, FOLD, 1)

    for head in range(HEADS):
        out[head * TOK : (head + 1) * TOK, :] = jnp.where(
            key < FOLD, folded(qa, ka, head), folded(qb, kb, head)
        ).astype(jnp.bfloat16)
    out[V_ROW : V_ROW + TOK, :] = va[...]
    out[V_ROW + TOK : END_ROW, :] = vb[...]
    lane = lax.broadcasted_iota(jnp.int32, (16, TOK), 1) & (FOLD - 1)
    row = lax.broadcasted_iota(jnp.int32, (16, TOK), 0)
    ends = end_of(jnp.where(row < 8, lane, lane + FOLD))
    out[END_ROW:, :] = ends.astype(jnp.float32).astype(jnp.bfloat16)


def attend(lengths, *operands):
    def whole(shape):
        return pl.BlockSpec(shape, lambda i: (0, 0))

    return pl.pallas_call(
        attend_kernel,
        out_shape=jax.ShapeDtypeStruct((ROWS, TOK), jnp.bfloat16),
        grid=(1,),
        in_specs=[pl.BlockSpec(memory_space=pltpu.SMEM)] + [whole(o.shape) for o in operands],
        out_specs=whole((ROWS, TOK)),
        compiler_params=pltpu.CompilerParams(vmem_limit_bytes=60 << 20),
        cost_estimate=pl.CostEstimate(flops=1, bytes_accessed=1, transcendentals=0),
    )(lengths, *operands)


def unpack_kernel(place, slot, column, block, *refs):
    out = refs[-1]
    ends = block[END_ROW:, :].astype(jnp.float32)
    end_low, end_high = ends[0:1, :].astype(jnp.int32), ends[8:9, :].astype(jnp.int32)
    key = lax.broadcasted_iota(jnp.int32, (TOK, TOK), 1) & (FOLD - 1)
    query = lax.broadcasted_iota(jnp.int32, (TOK, TOK), 0)
    low = jnp.where((key <= query) & (query <= end_low), 1.0, 0.0).astype(jnp.bfloat16)
    high = jnp.where((key + FOLD <= query) & (query <= end_high), 1.0, 0.0).astype(jnp.bfloat16)
    packed = block[:V_ROW, :].reshape(HEADS, TOK, TOK)
    weights = jnp.concatenate(
        [(packed * low[None]).reshape(V_ROW, TOK), (packed * high[None]).reshape(V_ROW, TOK)], axis=1
    )
    va, vb = block[V_ROW : V_ROW + TOK, :], block[V_ROW + TOK : END_ROW, :]
    none = jnp.zeros((FOLD, HD), jnp.bfloat16)
    values = jnp.concatenate(
        [
            jnp.concatenate([va[:FOLD], none], axis=1),
            jnp.concatenate([none, vb[:FOLD]], axis=1),
            jnp.concatenate([va[FOLD:], none], axis=1),
            jnp.concatenate([none, vb[FOLD:]], axis=1),
        ],
        axis=0,
    )
    mixed = jnp.dot(weights, values, preferred_element_type=jnp.float32).astype(jnp.bfloat16)
    for head in range(HEADS):
        part = mixed[head * TOK : (head + 1) * TOK, :]
        out[0, 0, 0, :, head * HD : (head + 1) * HD] = part[:, :HD]
        out[0, 1, 0, :, head * HD : (head + 1) * HD] = part[:, HD:]


def unpack(blocks, place, slot, column, before):
    count = blocks.shape[0] // ROWS
    return pl.pallas_call(
        unpack_kernel,
        out_shape=jax.ShapeDtypeStruct((4, 2, 2, TOK, 2 * HEADS * HD), jnp.bfloat16),
        grid_spec=pltpu.PrefetchScalarGridSpec(
            num_scalar_prefetch=3,
            grid=(count,),
            in_specs=[pl.BlockSpec((ROWS, TOK), lambda i, p, s, c: (i, 0))]
            + [pl.BlockSpec(memory_space=pl.ANY)] * len(before),
            out_specs=pl.BlockSpec(
                (1, 2, 1, TOK, HEADS * HD), lambda i, p, s, c: (p[i], 0, s[i], 0, c[i])
            ),
        ),
        input_output_aliases={4: 0} if before else {},
        compiler_params=pltpu.CompilerParams(vmem_limit_bytes=16 << 20),
        cost_estimate=pl.CostEstimate(flops=1, bytes_accessed=1, transcendentals=0),
    )(place, slot, column, blocks, *before)


def finish_kernel(
    column, sums, out_a, out_b, start, curvature, other_start, other_curvature, merged, residual
):
    norm = jnp.sum(sums[:, 0, :])
    step = norm / (jnp.sum(sums[:, 1, :]) / (16 * TOK) + damping * norm)
    midpoint = (out_a[...].astype(jnp.float32) + out_b[...].astype(jnp.float32)) * 0.5

    def write(begin, image):
        merged[...] = midpoint + step * begin
        residual[...] = begin - step * image

    @pl.when(pl.program_id(0) == 0)
    def _():
        write(start[...], curvature[...])

    @pl.when(pl.program_id(0) == 1)
    def _():
        write(other_start[...].astype(jnp.float32), other_curvature[...].astype(jnp.float32))


def finish(xl, sums, out_a, out_b, start, curvature, other_start, other_curvature):
    rows, width = other_start.shape
    tile = rows
    placed = pl.BlockSpec((tile, width), lambda i, r, x: (r, (i + x[0]) % 2))
    mine = pl.BlockSpec((tile, width), lambda i, r, x: (r, 0))
    other = pl.BlockSpec((tile, width), lambda i, r, x: (r, 0))
    shape = jax.ShapeDtypeStruct((rows, 2 * width), jnp.float32)
    return pl.pallas_call(
        finish_kernel,
        out_shape=[shape, shape],
        grid_spec=pltpu.PrefetchScalarGridSpec(
            num_scalar_prefetch=1,
            grid=(2, 1),
            in_specs=[pl.BlockSpec(sums.shape, lambda i, r, x: (0, 0, 0)), placed, placed, mine, mine, other, other],
            out_specs=[placed, placed],
        ),
        compiler_params=pltpu.CompilerParams(vmem_limit_bytes=56 << 20),
        cost_estimate=pl.CostEstimate(flops=1, bytes_accessed=1, transcendentals=0),
    )(
        xl.reshape(1),
        sums,
        out_a,
        out_b,
        start,
        curvature,
        other_start,
        other_curvature,
    )


def ring(value, axis, shift):
    return lax.ppermute(value, axis, [(i, (i + shift) % 4) for i in range(4)])


def swap(value, axis):
    return lax.ppermute(value, axis, [(0, 1), (1, 0)])


def plane_step(value, stage, hop):
    def index(y, x, c):
        return ((y * 2 + x // 2) * 2 + c) * 2 + x % 2

    pairs = []
    for y in range(4):
        for x in range(4):
            for c in range(2):
                along_x = (stage + c) % 2 == 0
                to = ((y, x ^ hop) if along_x else (y ^ hop, x)) + (c,)
                pairs.append((index(y, x, c), index(*to)))
    return lax.ppermute(value, PLANE, pairs)


tied = lax.optimization_barrier


def wide(part):
    return part.astype(jnp.float32)


def reduce_parts(partial):
    share = partial.shape[0] // 4
    half = share // 2
    return partial[share + half : 2 * share + half], partial[2 * share + half : 3 * share + half]


def reduce_start(partial):
    up, down = reduce_parts(partial)
    return ring(up, "z", 1), ring(down, "z", -1)


def reduce_next_parts(partial, up, down):
    share = partial.shape[0] // 4
    half = share // 2
    up_on = wide(partial[share : share + half]) + wide(up[half:])
    down_on = wide(partial[3 * share + half :]) + wide(down[:half])
    return up_on.astype(jnp.bfloat16), down_on.astype(jnp.bfloat16)


def reduce_next(partial, up, down):
    up_on, down_on = reduce_next_parts(partial, up, down)
    return ring(up_on, "z", 1), ring(down_on, "z", -1)


def reduce_end(partial, up, down, up_on, down_on):
    share = partial.shape[0] // 4
    half = share // 2
    return jnp.concatenate(
        [
            wide(partial[:half]) + wide(down[half:]) + wide(up_on),
            wide(partial[half:share]) + wide(up[:half]) + wide(down_on),
        ],
        axis=0,
    )


def spread_start(share):
    return ring(share, "z", 1), ring(share, "z", -1)


def spread_next(up, down):
    half = up.shape[0] // 2
    return ring(up[:half], "z", 1), ring(down[half:], "z", -1)


def spread_end(share, up, down, up_on, down_on):
    return jnp.concatenate([share, down, up_on, down_on, up], axis=0)


def by_share(pushed):
    return pushed.reshape(4, pushed.shape[0] // 4, pushed.shape[1])


def reduce_first(one, two):
    up = ring(jnp.concatenate([two[1], one[2]], axis=0), "z", 1)
    down = ring(jnp.concatenate([two[2], one[3]], axis=0), "z", -1)
    return up, down


def reduce_second(one, two, up, down):
    half = one.shape[1]
    up_on = (wide(one[1]) + wide(up[half:])).astype(jnp.bfloat16)
    down_on = (wide(two[3]) + wide(down[:half])).astype(jnp.bfloat16)
    return ring(up_on, "z", 1), ring(down_on, "z", -1)


def reduce_third(one, two, up, down, up_on, down_on):
    half = one.shape[1]
    return jnp.concatenate(
        [
            wide(one[0]) + wide(down[half:]) + wide(up_on),
            wide(two[0]) + wide(up[:half]) + wide(down_on),
        ],
        axis=0,
    )


def spread_first(share):
    return ring(share, "z", 1), ring(share, "z", -1)


def spread_second(up, down):
    half = up.shape[0] // 2
    return ring(up[:half], "z", 1), ring(down[half:], "z", -1)


def spread_third(share, up, down, up_on, down_on):
    half = share.shape[0] // 2
    return (
        jnp.concatenate([share[:half], down[:half], up_on, up[:half]], axis=0),
        jnp.concatenate([share[half:], down[half:], down_on, up[half:]], axis=0),
    )


def first_half(own, gap_mine, gap_sent):
    y, xh, c, z, xl = (lax.axis_index(axis) for axis in AXES)
    x = 2 * xh + xl
    hops = jnp.array(HOPS, jnp.int32)

    def add(array, core, hop, before):
        first, second = hops, jnp.full((4,), hop, jnp.int32)
        at_x = x ^ jnp.where(core == 0, first, second)
        at_y = y ^ jnp.where(core == 0, second, first)
        share = jnp.where(core == 0, (at_y % 2) * 2 + at_x // 2, at_y)
        slot = jnp.zeros((4,), jnp.int32) + core
        column = jnp.where(at_x % 2 == xl, 0, 1).astype(jnp.int32)
        return unpack(array, (share + 4 - z) % 4, slot, column, before)

    line = jnp.concatenate([own] + [plane_step(own, 0, hop) for hop in HOPS[1:]], axis=0)
    near, past = plane_step(line, 1, 1), plane_step(line, 1, 3)
    other_line = swap(line, "c")
    one = [add(line, c, 0, [])]
    one = [add(other_line, 1 - c, 0, one)]

    near, past, one, gap_sent = tied((near, past, one, gap_sent))
    far = plane_step(near, 1, 3)
    gap_got = swap(gap_sent, "xl")
    other_near, other_past = swap(near, "c"), swap(past, "c")
    one = [add(near, c, 1, one)]
    one = add(other_near, 1 - c, 1, one)
    two = [add(past, c, 3, [])]
    two = add(other_past, 1 - c, 3, two)
    gap_got, one, two = tied((gap_got, one, two))
    gap = jnp.concatenate([gap_mine, gap_got], axis=0)
    pushed_one = push(flat(one), gap)
    far, two, pushed_one = tied((far, two, pushed_one))
    first_one = reduce_start(pushed_one)
    other_far = swap(far, "c")
    two = add(far, c, 2, [two])
    two, other_far, first_one = tied((two, other_far, first_one))
    next_one = reduce_next(pushed_one, *first_one)
    two = add(other_far, 1 - c, 2, [two])
    pushed_two = push(flat(two), gap)

    sign = jnp.where(jnp.arange(4 * TOK) < 2 * TOK, 1.0, -1.0)[:, None]

    def rounded(*parts):
        return (sign * reduce_end(*parts)).astype(jnp.bfloat16)

    def both_ways(first, second):
        cut = first[0].shape[0]
        up = ring(jnp.concatenate([first[0], second[0]], axis=0), "z", 1)
        down = ring(jnp.concatenate([first[1], second[1]], axis=0), "z", -1)
        up, down = tied((up, down))
        return (up[:cut], down[:cut]), (up[cut:], down[cut:])

    pushed_two, next_one = tied((pushed_two, next_one))
    share_one = rounded(pushed_one, *first_one, *next_one)
    first_two, away_one = both_ways(reduce_parts(pushed_two), (share_one, share_one))
    half = share_one.shape[0] // 2
    next_two, on_one = both_ways(
        reduce_next_parts(pushed_two, *first_two), (away_one[0][:half], away_one[1][half:])
    )
    share_two = rounded(pushed_two, *first_two, *next_two)
    away_two = spread_start(share_two)
    start_one = pull_back(flat(one), spread_end(share_one, *away_one, *on_one))
    away_two, start_one = tied((away_two, start_one))
    on_two = spread_next(*away_two)
    start_two = pull_back(flat(two), spread_end(share_two, *away_two, *on_two))
    return flat(one), flat(two), start_one + start_two


def flat(chunk):
    return chunk.reshape(16 * TOK, 2 * HEADS * HD)


def pull_back(outputs, tangent):
    return lax.dot_general(
        outputs, tangent, (((0,), (0,)), ((), ())), preferred_element_type=jnp.float32
    )


def push(outputs, direction):
    return jnp.dot(outputs, direction, preferred_element_type=jnp.float32).astype(jnp.bfloat16)


def shards(queries_a, keys_a, values_a, queries_b, keys_b, values_b, out_a, out_b, lengths):
    xl = lax.axis_index("xl")
    token_total = 16 * TOK
    rows, width = out_a.shape[0], out_a.shape[1] // 2
    first = out_a.astype(jnp.float32)
    second = out_b.astype(jnp.float32)
    gap_low = ((first - second) * 0.5).astype(jnp.bfloat16)
    left, right = gap_low[:, :width], gap_low[:, width:]
    one, two, residual_start = first_half(
        attend(lengths, queries_a, keys_a, values_a, queries_b, keys_b, values_b),
        jnp.where(xl == 0, left, right),
        jnp.where(xl == 0, right, left),
    )
    residual_start = residual_start / token_total
    direction_low = residual_start.astype(jnp.bfloat16)

    pushed = by_share(push(one, direction_low)), by_share(push(two, direction_low))
    first = reduce_first(*pushed)
    other_start = swap(direction_low[rows:], "xl")
    residual_start, first = tied((residual_start, first))
    second = reduce_second(*pushed, *first)
    norm = jnp.sum(residual_start * residual_start, axis=0)
    norm, other_start, second = tied((norm, other_start, second))
    share = reduce_third(*pushed, *first, *second)
    low = share.astype(jnp.bfloat16)
    first = spread_first(low)
    totals = jnp.stack([norm, jnp.sum(share * share, axis=0)])
    totals = totals + swap(totals, "c")
    totals = totals + plane_step(totals, 0, 1)
    totals, first = tied((totals, first))
    second = spread_second(*first)
    totals = totals + plane_step(totals, 0, 3)
    totals, second = tied((totals, second))
    probe_one, probe_two = spread_third(low, *first, *second)
    image = pull_back(one, probe_one)
    totals = totals + plane_step(totals, 1, 1)
    totals, image = tied((totals, image))
    image = image + pull_back(two, probe_two)
    curvature = image / token_total + damping * residual_start
    sent = curvature[rows:].astype(jnp.bfloat16)
    other_curvature = swap(sent, "xl")
    totals = totals + plane_step(totals, 1, 3)
    totals = jnp.stack([totals] + [ring(totals, "z", k) for k in (1, 2, 3)])
    totals, other_curvature = tied((totals, other_curvature))
    return finish(
        xl, totals, out_a, out_b, residual_start, curvature, other_start, other_curvature
    )


def solution(mesh):
    fine = Mesh(mesh.devices.reshape(4, 2, 2, 4, 2), AXES)
    dp, tensor = ("y", "xh", "c"), ("z", "xl")
    tokens = P(dp, tensor)
    return jax.shard_map(
        shards,
        mesh=fine,
        in_specs=(tokens,) * 6 + (P(tensor, dp),) * 2 + (P(dp, None),),
        out_specs=(P(tensor, dp), P(tensor, dp)),
        check_vma=False,
    )
```
